32 devices in a mesh: sec: 16 (over z, x, core), blk: 2 (over y).
Axes of the slice: x: 2, y: 2, z: 4, core: 2. Of those that a mesh axis runs over, the one named last changes fastest.
Arguments:
- corner: bfloat16 [2048, 256], P('sec'), may hold values from -0.375 to 0.375
- edge_tiles: bfloat16 [2048, 16, 256], P(('sec', 'blk')), may hold values from -6 to 6
- projector: bfloat16 [2048, 16, 256], P(('sec', 'blk')), may hold values from -0.09375 to 0.09375
- sector_of: int32 [2048], P(('sec', 'blk')), may hold values from 0 to 7
Outputs:
- new_corner: float32 [2048, 256], P(('sec', 'blk'))
The draws below stay inside these ranges and needn't reach their ends.
All inputs are finite; a program needn't handle non-finite values.
Results may differ from the reference program's by a relative error of at most 0.0003.
Values may be sent and summed in bfloat16 or wider, within the bound.
No kernel may reach another device: no remote copies, remote signals or barrier semaphores. Data moves between devices by JAX's collectives and lax.ppermute only.
A program may use at most 64 MiB of HBM per device.

```python
import math
import jax
import jax.numpy as jnp
import numpy as np
from jax import lax

SD = 256
NS = 8
RB = 16
TILES_DEV = 64
TILES_ALL = 2048
N_SEC = 16
N_BLK = 2


def place_ends(array, own_key, smallest, high):
    place = [jax.random.randint(jax.random.fold_in(own_key, axis), (), 0, length) for axis, length in enumerate(array.shape)]
    main_axis = array.shape.index(max(array.shape))
    next_to = place[:main_axis] + [(place[main_axis] + 1) % array.shape[main_axis]] + place[main_axis + 1:]
    return array.at[tuple(place)].set(smallest).at[tuple(next_to)].set(high)


def block_scale(key, extent, split, low, high):
    def one(dim, parts):
        draws = jax.random.uniform(jax.random.fold_in(jax.random.fold_in(key, 6), dim), (parts,), jnp.float32, low / len(split), high / len(split))
        return jnp.repeat(jnp.exp(draws), extent[dim] // parts).reshape((-1,) + (1,) * (len(extent) - dim - 1))

    level = one(*split[0])
    for cut in split[1:]:
        level = level * one(*cut)
    return level


def rank_bounds(number_of, skew):
    portions = [(1 << 20) // math.isqrt(rank ** skew) + 1 for rank in range(1, number_of + 1)]
    scale = 1 + sum(portions) // (1 << 30)
    return np.cumsum(np.array([max(1, weight // scale) for weight in portions]))


def ranked(stream_key, shape, amount, lean):
    listing = rank_bounds(amount, lean)
    ticket = jax.random.randint(jax.random.fold_in(stream_key, 1), shape, 0, int(listing[amount - 1]))
    standing = jnp.searchsorted(jnp.asarray(listing, jnp.int32), ticket, side="right")
    return jax.random.permutation(jax.random.fold_in(stream_key, 2), amount)[standing].astype(jnp.int32)


def gaussian(rng, extent, deviation, limit, shards=(), held_as=jnp.bfloat16):
    entries = jax.random.normal(rng, extent, jnp.float32) * deviation
    if len(shards) > 0:
        entries = block_scale(rng, extent, shards, -0.22, 0.18) * entries
    return jnp.clip(entries, min=-limit, max=limit).astype(held_as)


def setup_inputs(seed: int = 0) -> dict:
    key_list = jax.random.split(jax.random.key(seed), 5)
    corner = gaussian(key_list[0], (NS * SD, SD), SD ** -0.5, 0.375, ((0, 16),))
    edge_tiles = gaussian(key_list[1], (TILES_ALL, RB, SD), 1.0, 6.0, ((0, 32),))
    projector = gaussian(key_list[2], (TILES_ALL, RB, SD), (TILES_ALL * RB // NS) ** -0.5, 0.09375, ((0, 32),))
    sector_of = place_ends(ranked(key_list[3], (TILES_ALL,), NS, 2), jax.random.fold_in(key_list[3], 3), 0, NS - 1).astype(jnp.int32)
    return {"corner": corner, "edge_tiles": edge_tiles, "projector": projector, "sector_of": sector_of}


def reference(corner, edge_tiles, projector, sector_of):
    per_peer = TILES_DEV // N_SEC
    paired = projector.reshape(N_SEC, N_BLK, N_SEC, per_peer, RB, SD)
    paired = paired.transpose(2, 1, 0, 3, 4, 5).reshape(TILES_ALL, RB, SD)
    blocks3 = corner.reshape(NS, SD, SD)
    labels = jnp.arange(NS, dtype=jnp.int32)

    def advance(running, group_item):
        tile_group, proj_group, sector_group = group_item
        chosen = jnp.take(blocks3, sector_group, axis=0).astype(jnp.float32)
        image = jnp.einsum('trs,tsu->tru', tile_group.astype(jnp.float32), chosen, precision=lax.Precision.HIGHEST)
        contrib = jnp.einsum('trs,tru->tsu', proj_group.astype(jnp.float32), image, precision=lax.Precision.HIGHEST)
        indicator = (sector_group[:, None] == labels[None, :]).astype(jnp.float32)
        return running + jnp.einsum('tb,tsu->bsu', indicator, contrib, precision=lax.Precision.HIGHEST), None

    items = (edge_tiles.reshape(-1, TILES_DEV, RB, SD), paired.reshape(-1, TILES_DEV, RB, SD), sector_of.reshape(-1, TILES_DEV))
    summed, _ = lax.scan(advance, jnp.zeros((NS, SD, SD), jnp.float32), items)
    return summed.reshape(NS * SD, SD)
```

```python
import functools

import jax
import jax.numpy as jnp
from jax import lax
from jax.experimental import pallas as pl
from jax.experimental.pallas import tpu as pltpu
from jax.sharding import PartitionSpec as P

VMEM_LIMIT = 48 * 1024 * 1024


def transpose_kernel(p_ref, o_ref):
    groups, rows, _ = p_ref.shape
    for g in range(groups):
        o_ref[g] = p_ref[g].T


def transpose_rows(p3):
    groups, rows, width = p3.shape
    if rows % 128 or width % 128:
        return jnp.swapaxes(p3, 1, 2)
    return pl.pallas_call(
        transpose_kernel,
        out_shape=jax.ShapeDtypeStruct((groups, width, rows), p3.dtype),
        compiler_params=pltpu.CompilerParams(vmem_limit_bytes=VMEM_LIMIT),
    )(p3)


def fold_kernel(sector_count, lane_ref, slab_ref, *refs):
    edge_refs, out_ref = refs[:-1], refs[-1]
    peers, _, depth = lane_ref.shape
    blk_count = slab_ref.shape[1]
    step = edge_refs[0].shape[1]
    for d in range(peers):
        left = jnp.concatenate([slab_ref[d, j] for j in range(blk_count)], axis=1)
        lane = lane_ref[d]
        rows = []
        for b in range(sector_count):
            chosen = (lane == b).astype(jnp.float32).astype(left.dtype)
            rows.append(left * chosen)
        right = jnp.concatenate([e[d] for e in edge_refs], axis=0)
        part = jnp.dot(
            jnp.concatenate(rows, axis=0), right, preferred_element_type=jnp.float32
        ).reshape(out_ref.shape)
        if d == 0:
            out_ref[...] = part
        else:
            out_ref[...] += part


def fold_tiles(slabs, edges, lanes, sector_count):
    peers, blk_count, cols, depth = slabs.shape
    width = edges[0].shape[2]
    if depth % 128 or cols % 16 or edges[0].shape[1] % 16:
        left = jnp.moveaxis(slabs, 2, 1).reshape(peers, 1, cols, blk_count * depth)
        labels = jnp.arange(sector_count, dtype=jnp.int32)[None, :, None, None]
        left = left * (lanes[:, :, None, :] == labels).astype(left.dtype)
        right = jnp.concatenate(edges, axis=1)
        return jnp.einsum("dbsk,dku->bsu", left, right, preferred_element_type=jnp.float32)
    return pl.pallas_call(
        functools.partial(fold_kernel, sector_count),
        out_shape=jax.ShapeDtypeStruct((sector_count, cols, width), jnp.float32),
        compiler_params=pltpu.CompilerParams(vmem_limit_bytes=VMEM_LIMIT),
    )(lanes, slabs, *edges)


def pairwise(first, second, odd):
    return jnp.where(odd, second, first), jnp.where(odd, first, second)


def local(corner, edge_tiles, projector, sector_of):
    sec_count, blk_count = lax.axis_size("sec"), lax.axis_size("blk")
    me, my_blk = lax.axis_index("sec"), lax.axis_index("blk")
    tile_count, tile_rows, width = edge_tiles.shape
    columns = sec_count // 2
    per_peer = tile_count // sec_count
    slab_depth = per_peer * tile_rows
    corner_rows = corner.shape[0]
    sector_count = corner_rows * sec_count // width
    out_rows = corner_rows // blk_count
    spread = columns // sector_count
    sibling = [(i, i ^ 1) for i in range(sec_count)]

    def turn(array, by):
        return lax.ppermute(array, "blk", [(j, (j + by) % blk_count) for j in range(blk_count)])

    edges3 = edge_tiles.reshape(sec_count, slab_depth, width)
    edge_turns = [edges3] + [turn(edges3, k) for k in range(1, blk_count)]
    sector_turns = [sector_of] + [turn(sector_of, k) for k in range(1, blk_count)]
    edge_pairs = [(e, lax.ppermute(e, "sec", sibling)) for e in edge_turns]
    sector_all = jnp.stack(sector_turns)
    sector_both = jnp.stack([sector_all, lax.ppermute(sector_all, "sec", sibling)])

    slabs = transpose_rows(projector.reshape(columns, 2 * slab_depth, width))
    slabs = slabs.reshape(columns, spread, 2, blk_count, out_rows, 2 * slab_depth)
    slabs = jnp.moveaxis(slabs, 1, 3)
    slabs = slabs.reshape(sec_count * blk_count, spread * out_rows, 2 * slab_depth)
    arrived = lax.all_to_all(slabs, ("sec", "blk"), split_axis=0, concat_axis=0, tiled=True)
    arrived = arrived.reshape(sec_count, blk_count, spread * out_rows, 2 * slab_depth)

    odd = me % 2 == 1
    turned = (my_blk - jnp.arange(blk_count)) % blk_count
    edges = []
    for j in range(blk_count):
        own, other = edge_pairs[0]
        for k in range(1, blk_count):
            own = jnp.where((my_blk - k) % blk_count == j, edge_pairs[k][0], own)
            other = jnp.where((my_blk - k) % blk_count == j, edge_pairs[k][1], other)
        edges.extend(pairwise(own, other, odd))
    sector_both = jnp.where(odd, sector_both[::-1], sector_both)
    sector_both = jnp.take(sector_both, turned, axis=1)
    lanes = jnp.moveaxis(sector_both.reshape(2, blk_count, sec_count, per_peer), 2, 0)
    lanes = jnp.swapaxes(lanes, 1, 2)
    lanes = jnp.repeat(lanes.reshape(sec_count, 1, -1), tile_rows, axis=2)

    partial = fold_tiles(arrived, edges, lanes, sector_count)
    partial = partial.reshape(columns, out_rows, width)
    groups = [[2 * n + c for n in range(columns)] for c in range(2)]
    received = lax.all_to_all(
        partial, "sec", split_axis=0, concat_axis=0, tiled=True, axis_index_groups=groups
    )
    rows = jnp.sum(received, axis=0)

    share = 2 * spread
    place = me % share
    block = jnp.zeros((share, corner_rows, width), corner.dtype)
    for k in range(share):
        ring = [(i, i // share * share + (i % share + k) % share) for i in range(sec_count)]
        piece = corner if k == 0 else lax.ppermute(corner, "sec", ring)
        block = lax.dynamic_update_index_in_dim(block, piece, (place - k) % share, 0)
    block = block.reshape(width, width)
    high = lax.reduce_precision(rows, exponent_bits=8, mantissa_bits=7)
    low = (rows - high).astype(jnp.bfloat16)
    both = jnp.dot(
        jnp.concatenate([high.astype(jnp.bfloat16), low], axis=0), block, preferred_element_type=jnp.float32
    )
    return both[:out_rows] + both[out_rows:]


def solution(mesh):
    in_specs = (
        P("sec", None),
        P(("sec", "blk"), None, None),
        P(("sec", "blk"), None, None),
        P(("sec", "blk")),
    )
    out_specs = P(("sec", "blk"), None)
    return jax.shard_map(local, mesh=mesh, in_specs=in_specs, out_specs=out_specs, check_vma=False)
```

```python
import functools

import jax
import jax.numpy as jnp
from jax import lax
from jax.experimental import pallas as pl
from jax.experimental.pallas import tpu as pltpu
from jax.sharding import PartitionSpec as P

VMEM_LIMIT = 48 * 1024 * 1024
TOP = 14
NOTE_ROWS = 8


def slab_kernel(p_hbm, o_hbm, p_ref, o_ref, in_sems, out_sems):
    pairs, rows, width = p_ref.shape
    cols, depth = o_ref.shape[-1] // 2, rows // 2
    blk_count = o_ref.shape[1] // 2
    arrive = [pltpu.make_async_copy(p_hbm.at[g], p_ref.at[g], in_sems.at[g]) for g in range(pairs)]
    leave = [pltpu.make_async_copy(o_ref.at[g], o_hbm.at[g], out_sems.at[g]) for g in range(pairs)]
    for copy in arrive:
        copy.start()
    for g in range(pairs):
        arrive[g].wait()
        for c in range(2):
            own = p_ref[g, c * depth : (c + 1) * depth, :]
            other = p_ref[g, (1 - c) * depth : (2 - c) * depth, :]
            for j in range(blk_count):
                k = (c * blk_count + j) * cols
                o_ref[g, c * blk_count + j] = jnp.concatenate(
                    [own[:, k : k + cols], other[:, k : k + cols]], axis=1
                )
        leave[g].start()
    for copy in leave:
        copy.wait()


def make_slabs(projector, pairs, blk_count, out_rows):
    width = projector.shape[-1]
    p3 = projector.reshape(pairs, -1, width)
    depth = p3.shape[1] // 2
    spread = width // (2 * blk_count * out_rows)
    shape = (pairs, 2 * blk_count, depth, 2 * spread * out_rows)
    if depth % 16 or shape[3] % 128 or spread != 1:
        split = p3.reshape(pairs, 2, depth, spread, 2, blk_count, out_rows)
        split = jnp.stack([split[:, :, :, :, 0], split[:, ::-1, :, :, 1]], axis=1)
        return split.transpose(0, 1, 5, 3, 2, 4, 6).reshape(shape)
    in_hbm = pl.BlockSpec(memory_space=pltpu.HBM)
    return pl.pallas_call(
        slab_kernel,
        out_shape=jax.ShapeDtypeStruct(shape, p3.dtype),
        in_specs=[in_hbm],
        out_specs=in_hbm,
        scratch_shapes=[
            pltpu.VMEM(p3.shape, p3.dtype),
            pltpu.VMEM(shape, p3.dtype),
            pltpu.SemaphoreType.DMA((pairs,)),
            pltpu.SemaphoreType.DMA((pairs,)),
        ],
    )(p3)


def exponent_of(largest):
    return jnp.round(jnp.log2(jnp.clip(largest, 2.0**-100, 2.0**100)))


def fold_kernel(sector_count, out_rows, blk_ref, lane_ref, slab_ref, *refs):
    edge_refs, out_ref, total_ref = refs[:-2], refs[-2], refs[-1]
    peers, blk_count, _, cols = slab_ref.shape
    cols = cols // 2
    order = [lax.rem(blk_ref[0] + blk_count - k, blk_count) for k in range(blk_count)]
    for d in range(peers):
        left = jnp.concatenate([slab_ref[d, j] for j in order], axis=0).T
        left = jnp.concatenate([left[:cols], left[cols:]], axis=1)
        lane = lane_ref[d]
        rows = []
        for b in range(sector_count):
            chosen = (lane == b).astype(jnp.float32).astype(left.dtype)
            rows.append(left * chosen)
        right = jnp.concatenate([e[d] for e in edge_refs], axis=0)
        part = jnp.dot(jnp.concatenate(rows, axis=0), right, preferred_element_type=jnp.float32)
        if d == 0:
            total_ref[...] = part
        else:
            total_ref[...] += part
    exponent = exponent_of(jnp.max(jnp.abs(total_ref[...]), axis=(0, 1), keepdims=True))
    scale = jnp.exp2(TOP - exponent)
    lanes = out_ref.shape[2]
    parts = total_ref.shape[1] // lanes
    dests = out_ref.shape[0]
    for n in range(dests):
        place = (n + dests // 2) % dests
        for k in range(parts):
            out_ref[place, k * out_rows : (k + 1) * out_rows] = (
                total_ref[n * out_rows : (n + 1) * out_rows, k * lanes : (k + 1) * lanes] * scale
            )
        out_ref[place, parts * out_rows :] = jnp.broadcast_to(exponent, (NOTE_ROWS, lanes))


def fold_tiles(slabs, edges, lanes, my_blk, sector_count, out_rows):
    peers, blk_count, depth, cols = slabs.shape
    cols = cols // 2
    width = edges[0].shape[2]
    dests = sector_count * cols // out_rows
    part_width = 128 if width % 128 == 0 else width
    parts = width // part_width
    shape = (dests, parts * out_rows + NOTE_ROWS, part_width)
    if depth * blk_count % 128 or depth % 16 or cols % 64 or out_rows % 16:
        order = (my_blk - jnp.arange(blk_count)) % blk_count
        left = jnp.take(slabs, order, axis=1).reshape(peers, blk_count, depth, 2, cols)
        left = left.transpose(0, 4, 3, 1, 2).reshape(peers, 1, cols, 2 * blk_count * depth)
        labels = jnp.arange(sector_count, dtype=jnp.int32)[None, :, None, None]
        left = left * (lanes[:, :, None, :] == labels).astype(left.dtype)
        right = jnp.concatenate(edges, axis=1)
        total = jnp.einsum("dbsk,dku->bsu", left, right, preferred_element_type=jnp.float32)
        exponent = exponent_of(jnp.max(jnp.abs(total)))
        total = total.reshape(dests, out_rows, parts, part_width) * jnp.exp2(TOP - exponent)
        total = jnp.swapaxes(total, 1, 2).reshape(dests, parts * out_rows, part_width)
        note = jnp.full((dests, NOTE_ROWS, part_width), exponent)
        return jnp.roll(jnp.concatenate([total, note], axis=1), dests // 2, axis=0)
    in_vmem = pl.BlockSpec(memory_space=pltpu.VMEM)
    return pl.pallas_call(
        functools.partial(fold_kernel, sector_count, out_rows),
        out_shape=jax.ShapeDtypeStruct(shape, jnp.float32),
        in_specs=[pl.BlockSpec(memory_space=pltpu.SMEM)] + [in_vmem] * (2 + len(edges)),
        out_specs=in_vmem,
        scratch_shapes=[pltpu.VMEM((sector_count * cols, width), jnp.float32)],
        compiler_params=pltpu.CompilerParams(vmem_limit_bytes=VMEM_LIMIT),
    )(my_blk.reshape(1), lanes, slabs, *edges)


def local(corner, edge_tiles, projector, sector_of):
    sec_count, blk_count = lax.axis_size("sec"), lax.axis_size("blk")
    me, my_blk = lax.axis_index("sec"), lax.axis_index("blk")
    tile_count, tile_rows, width = edge_tiles.shape
    columns = sec_count // 2
    per_peer = tile_count // sec_count
    slab_depth = per_peer * tile_rows
    corner_rows = corner.shape[0]
    sector_count = corner_rows * sec_count // width
    out_rows = corner_rows // blk_count
    spread = columns // sector_count
    sibling = [(i, i ^ 1) for i in range(sec_count)]

    def turn(array, by):
        return lax.ppermute(array, "blk", [(j, (j + by) % blk_count) for j in range(blk_count)])

    edges3 = edge_tiles.reshape(sec_count, slab_depth, width)
    edge_turns = [edges3] + [turn(edges3, k) for k in range(1, blk_count)]
    sectors = jnp.stack([sector_of] + [turn(sector_of, k) for k in range(1, blk_count)])
    lanes = jnp.stack([sectors, lax.ppermute(sectors, "sec", sibling)])
    lanes = jnp.moveaxis(lanes.reshape(2 * blk_count, sec_count, per_peer), 1, 0)
    lanes = jnp.repeat(lanes.reshape(sec_count, 1, -1), tile_rows, axis=2)
    others = [lax.ppermute(edges3, "sec", sibling)]
    edge_turns, lanes = lax.optimization_barrier((edge_turns, lanes))
    others += [lax.ppermute(e, "sec", sibling) for e in edge_turns[1:]]

    slabs = make_slabs(projector, columns, blk_count, out_rows)
    slabs = slabs.reshape(sec_count * blk_count, slab_depth, 2 * spread * out_rows)
    arrived = lax.all_to_all(slabs, ("sec", "blk"), split_axis=0, concat_axis=0, tiled=True)
    arrived = arrived.reshape(sec_count, blk_count, slab_depth, 2 * spread * out_rows)

    partial = fold_tiles(arrived, edge_turns + others, lanes, my_blk, sector_count, out_rows)
    middle = [(n - columns // 2) % columns for n in range(columns)]
    groups = [[2 * n + c for n in middle] for c in range(2)]
    received = lax.all_to_all(
        partial.astype(jnp.float16),
        "sec",
        split_axis=0,
        concat_axis=0,
        tiled=True,
        axis_index_groups=groups,
    ).astype(jnp.float32)
    scales = jnp.exp2(received[:, -1:, :1] - TOP)
    rows = jnp.sum(received[:, :-NOTE_ROWS] * scales, axis=0)
    rows = jnp.concatenate(jnp.split(rows, rows.shape[0] // out_rows), axis=1)

    share = 2 * spread
    place = me % share
    block = jnp.zeros((share, corner_rows, width), corner.dtype)
    for k in range(share):
        ring = [(i, i // share * share + (i % share + k) % share) for i in range(sec_count)]
        piece = corner if k == 0 else lax.ppermute(corner, "sec", ring)
        block = lax.dynamic_update_index_in_dim(block, piece, (place - k) % share, 0)
    block = block.reshape(width, width)
    high = lax.reduce_precision(rows, exponent_bits=8, mantissa_bits=7)
    both = jnp.concatenate([high, rows - high], axis=0).astype(jnp.bfloat16)
    both = jnp.dot(both, block, preferred_element_type=jnp.float32)
    return both[:out_rows] + both[out_rows:]


def solution(mesh):
    in_specs = (
        P("sec", None),
        P(("sec", "blk"), None, None),
        P(("sec", "blk"), None, None),
        P(("sec", "blk")),
    )
    out_specs = P(("sec", "blk"), None)
    return jax.shard_map(local, mesh=mesh, in_specs=in_specs, out_specs=out_specs, check_vma=False)
```

```python
import functools

import jax
import jax.numpy as jnp
import numpy as np
from jax import lax
from jax.experimental import pallas as pl
from jax.experimental.pallas import tpu as pltpu
from jax.sharding import PartitionSpec as P

VMEM_LIMIT = 48 * 1024 * 1024
TOP = 14
NOTE_ROWS = 8


def ring_of(count):
    stride = 3 if count % 3 else 1
    return [-stride * n % count for n in range(count)]


def slab_kernel(p_hbm, o_hbm, p_ref, o_ref, in_sems, out_sems):
    pairs = p_ref.shape[0]
    dests, depth, cols = o_ref.shape
    per_pair, cols = dests // pairs, cols // 2
    parts = [pl.ds(h * pairs // 2, pairs // 2) for h in range(2)]
    arrive = [pltpu.make_async_copy(p_hbm.at[h], p_ref.at[h], in_sems.at[k]) for k, h in enumerate(parts)]
    parts = [pl.ds(h * dests // 2, dests // 2) for h in range(2)]
    leave = [pltpu.make_async_copy(o_ref.at[h], o_hbm.at[h], out_sems.at[k]) for k, h in enumerate(parts)]
    for copy in arrive:
        copy.start()
    for copy in arrive:
        copy.wait()
    for place, n in enumerate(ring_of(dests)):
        g, j = divmod(n, per_pair)
        c = 2 * j // per_pair
        own = p_ref[g, c * depth : (c + 1) * depth, j * cols : (j + 1) * cols]
        other = p_ref[g, (1 - c) * depth : (2 - c) * depth, j * cols : (j + 1) * cols]
        o_ref[place] = jnp.concatenate([own, other], axis=1)
        if place + 1 == dests // 2:
            leave[0].start()
    leave[1].start()
    for copy in leave:
        copy.wait()


def make_slabs(projector, pairs, blk_count, out_rows):
    width = projector.shape[-1]
    p3 = projector.reshape(pairs, -1, width)
    depth = p3.shape[1] // 2
    spread = width // (2 * blk_count * out_rows)
    dests = pairs * 2 * blk_count
    shape = (dests, depth, 2 * spread * out_rows)
    if depth % 16 or shape[2] % 128 or spread != 1 or pairs % 2:
        split = p3.reshape(pairs, 2, depth, spread, 2, blk_count, out_rows)
        split = jnp.stack([split[:, :, :, :, 0], split[:, ::-1, :, :, 1]], axis=1)
        slabs = split.transpose(0, 1, 5, 3, 2, 4, 6).reshape(shape)
        return jnp.take(slabs, np.array(ring_of(dests)), axis=0)
    in_hbm = pl.BlockSpec(memory_space=pltpu.HBM)
    return pl.pallas_call(
        slab_kernel,
        out_shape=jax.ShapeDtypeStruct(shape, p3.dtype),
        in_specs=[in_hbm],
        out_specs=in_hbm,
        scratch_shapes=[
            pltpu.VMEM(p3.shape, p3.dtype),
            pltpu.VMEM(shape, p3.dtype),
            pltpu.SemaphoreType.DMA((2,)),
            pltpu.SemaphoreType.DMA((2,)),
        ],
    )(p3)


def exponent_of(largest):
    return jnp.round(jnp.log2(jnp.clip(largest, 2.0**-100, 2.0**100)))


def fold_kernel(sector_count, out_rows, blk_ref, lane_ref, slab_ref, *refs):
    edge_refs, out_ref, total_ref = refs[:-2], refs[-2], refs[-1]
    peers = lane_ref.shape[0]
    sources, _, cols = slab_ref.shape
    cols, blk_count = cols // 2, sources // peers
    place = {n: k for k, n in enumerate(ring_of(sources))}
    order = [lax.rem(blk_ref[0] + blk_count - k, blk_count) for k in range(blk_count)]
    for d in range(peers):
        places = [place[d * blk_count + j] for j in range(blk_count)]
        left = []
        for j in order:
            n = places[0]
            for k in range(1, blk_count):
                n = jnp.where(j == k, places[k], n)
            left.append(slab_ref[n])
        left = jnp.concatenate(left, axis=0).T
        left = jnp.concatenate([left[:cols], left[cols:]], axis=1)
        lane = lane_ref[d]
        rows = []
        for b in range(sector_count):
            chosen = (lane == b).astype(jnp.float32).astype(left.dtype)
            rows.append(left * chosen)
        right = jnp.concatenate([e[d] for e in edge_refs], axis=0)
        part = jnp.dot(jnp.concatenate(rows, axis=0), right, preferred_element_type=jnp.float32)
        if d == 0:
            total_ref[...] = part
        else:
            total_ref[...] += part
    exponent = exponent_of(jnp.max(jnp.abs(total_ref[...]), axis=(0, 1), keepdims=True))
    scale = jnp.exp2(TOP - exponent)
    lanes = out_ref.shape[2]
    parts = total_ref.shape[1] // lanes
    dests = out_ref.shape[0]
    for n in range(dests):
        place = (n + dests // 2) % dests
        for k in range(parts):
            out_ref[place, k * out_rows : (k + 1) * out_rows] = (
                total_ref[n * out_rows : (n + 1) * out_rows, k * lanes : (k + 1) * lanes] * scale
            )
        out_ref[place, parts * out_rows :] = jnp.broadcast_to(exponent, (NOTE_ROWS, lanes))


def fold_tiles(slabs, edges, lanes, my_blk, sector_count, out_rows):
    sources, depth, cols = slabs.shape
    peers, _, width = edges[0].shape
    cols, blk_count = cols // 2, sources // peers
    dests = sector_count * cols // out_rows
    part_width = 128 if width % 128 == 0 else width
    parts = width // part_width
    shape = (dests, parts * out_rows + NOTE_ROWS, part_width)
    if depth * blk_count % 128 or depth % 16 or cols % 64 or out_rows % 16:
        order = (my_blk - jnp.arange(blk_count)) % blk_count
        left = jnp.take(slabs, np.argsort(ring_of(sources)), axis=0)
        left = left.reshape(peers, blk_count, depth, 2, cols)
        left = jnp.take(left, order, axis=1)
        left = left.transpose(0, 4, 3, 1, 2).reshape(peers, 1, cols, 2 * blk_count * depth)
        labels = jnp.arange(sector_count, dtype=jnp.int32)[None, :, None, None]
        left = left * (lanes[:, :, None, :] == labels).astype(left.dtype)
        right = jnp.concatenate(edges, axis=1)
        total = jnp.einsum("dbsk,dku->bsu", left, right, preferred_element_type=jnp.float32)
        exponent = exponent_of(jnp.max(jnp.abs(total)))
        total = total.reshape(dests, out_rows, parts, part_width) * jnp.exp2(TOP - exponent)
        total = jnp.swapaxes(total, 1, 2).reshape(dests, parts * out_rows, part_width)
        note = jnp.full((dests, NOTE_ROWS, part_width), exponent)
        return jnp.roll(jnp.concatenate([total, note], axis=1), dests // 2, axis=0)
    in_vmem = pl.BlockSpec(memory_space=pltpu.VMEM)
    return pl.pallas_call(
        functools.partial(fold_kernel, sector_count, out_rows),
        out_shape=jax.ShapeDtypeStruct(shape, jnp.float32),
        in_specs=[pl.BlockSpec(memory_space=pltpu.SMEM)] + [in_vmem] * (2 + len(edges)),
        out_specs=in_vmem,
        scratch_shapes=[pltpu.VMEM((sector_count * cols, width), jnp.float32)],
        compiler_params=pltpu.CompilerParams(vmem_limit_bytes=VMEM_LIMIT),
    )(my_blk.reshape(1), lanes, slabs, *edges)


def local(corner, edge_tiles, projector, sector_of):
    sec_count, blk_count = lax.axis_size("sec"), lax.axis_size("blk")
    me, my_blk = lax.axis_index("sec"), lax.axis_index("blk")
    tile_count, tile_rows, width = edge_tiles.shape
    columns = sec_count // 2
    per_peer = tile_count // sec_count
    slab_depth = per_peer * tile_rows
    corner_rows = corner.shape[0]
    sector_count = corner_rows * sec_count // width
    out_rows = corner_rows // blk_count
    spread = columns // sector_count
    sibling = [(i, i ^ 1) for i in range(sec_count)]

    def turn(array, by):
        return lax.ppermute(array, "blk", [(j, (j + by) % blk_count) for j in range(blk_count)])

    edges3 = edge_tiles.reshape(sec_count, slab_depth, width)
    edge_turns = [edges3] + [turn(edges3, k) for k in range(1, blk_count)]
    sectors = jnp.stack([sector_of] + [turn(sector_of, k) for k in range(1, blk_count)])
    lanes = jnp.stack([sectors, lax.ppermute(sectors, "sec", sibling)])
    lanes = jnp.moveaxis(lanes.reshape(2 * blk_count, sec_count, per_peer), 1, 0)
    lanes = jnp.repeat(lanes.reshape(sec_count, 1, -1), tile_rows, axis=2)
    others = [lax.ppermute(edges3, "sec", sibling)]
    edge_turns, lanes = lax.optimization_barrier((edge_turns, lanes))
    others += [lax.ppermute(e, "sec", sibling) for e in edge_turns[1:]]

    slabs = make_slabs(projector, columns, blk_count, out_rows)
    arrived = lax.all_to_all(
        slabs,
        ("sec", "blk"),
        split_axis=0,
        concat_axis=0,
        tiled=True,
        axis_index_groups=[ring_of(sec_count * blk_count)],
    )

    partial = fold_tiles(arrived, edge_turns + others, lanes, my_blk, sector_count, out_rows)
    middle = [(n - columns // 2) % columns for n in range(columns)]
    groups = [[2 * n + c for n in middle] for c in range(2)]
    received = lax.all_to_all(
        partial.astype(jnp.float16),
        "sec",
        split_axis=0,
        concat_axis=0,
        tiled=True,
        axis_index_groups=groups,
    ).astype(jnp.float32)
    scales = jnp.exp2(received[:, -1:, :1] - TOP)
    rows = jnp.sum(received[:, :-NOTE_ROWS] * scales, axis=0)
    rows = jnp.concatenate(jnp.split(rows, rows.shape[0] // out_rows), axis=1)

    share = 2 * spread
    place = me % share
    block = jnp.zeros((share, corner_rows, width), corner.dtype)
    for k in range(share):
        ring = [(i, i // share * share + (i % share + k) % share) for i in range(sec_count)]
        piece = corner if k == 0 else lax.ppermute(corner, "sec", ring)
        block = lax.dynamic_update_index_in_dim(block, piece, (place - k) % share, 0)
    block = block.reshape(width, width)
    high = lax.reduce_precision(rows, exponent_bits=8, mantissa_bits=7)
    both = jnp.concatenate([high, rows - high], axis=1).astype(jnp.bfloat16)
    twice = jnp.concatenate([block, block], axis=0)
    return jnp.dot(both, twice, preferred_element_type=jnp.float32)


def solution(mesh):
    in_specs = (
        P("sec", None),
        P(("sec", "blk"), None, None),
        P(("sec", "blk"), None, None),
        P(("sec", "blk")),
    )
    out_specs = P(("sec", "blk"), None)
    return jax.shard_map(local, mesh=mesh, in_specs=in_specs, out_specs=out_specs, check_vma=False)
```

```python
import functools

import jax
import jax.numpy as jnp
import numpy as np
from jax import lax
from jax.experimental import pallas as pl
from jax.experimental.pallas import tpu as pltpu
from jax.sharding import PartitionSpec as P

VMEM_LIMIT = 48 * 1024 * 1024
TOP = 14
NOTE_ROWS = 8


def ring_of(count):
    stride = 3 if count % 3 else 1
    return [(count // 2 - stride * n) % count for n in range(count)]


def slab_kernel(p_hbm, o_hbm, p_ref, o_ref, in_sems, out_sems):
    pairs = p_ref.shape[0]
    dests, depth, cols = o_ref.shape
    per_pair, cols = dests // pairs, cols // 2
    parts = [pl.ds(h * pairs // 2, pairs // 2) for h in range(2)]
    arrive = [pltpu.make_async_copy(p_hbm.at[h], p_ref.at[h], in_sems.at[k]) for k, h in enumerate(parts)]
    parts = [pl.ds(h * dests // 2, dests // 2) for h in range(2)]
    leave = [pltpu.make_async_copy(o_ref.at[h], o_hbm.at[h], out_sems.at[k]) for k, h in enumerate(parts)]
    for copy in arrive:
        copy.start()
    for copy in arrive:
        copy.wait()
    for place, n in enumerate(ring_of(dests)):
        g, j = divmod(n, per_pair)
        c = 2 * j // per_pair
        own = p_ref[g, c * depth : (c + 1) * depth, j * cols : (j + 1) * cols]
        other = p_ref[g, (1 - c) * depth : (2 - c) * depth, j * cols : (j + 1) * cols]
        o_ref[place] = jnp.concatenate([own, other], axis=1)
        if place + 1 == dests // 2:
            leave[0].start()
    leave[1].start()
    for copy in leave:
        copy.wait()


def make_slabs(projector, pairs, blk_count, out_rows):
    width = projector.shape[-1]
    p3 = projector.reshape(pairs, -1, width)
    depth = p3.shape[1] // 2
    spread = width // (2 * blk_count * out_rows)
    dests = pairs * 2 * blk_count
    shape = (dests, depth, 2 * spread * out_rows)
    if depth % 16 or shape[2] % 128 or spread != 1 or pairs % 2:
        split = p3.reshape(pairs, 2, depth, spread, 2, blk_count, out_rows)
        split = jnp.stack([split[:, :, :, :, 0], split[:, ::-1, :, :, 1]], axis=1)
        slabs = split.transpose(0, 1, 5, 3, 2, 4, 6).reshape(shape)
        return jnp.take(slabs, np.array(ring_of(dests)), axis=0)
    in_hbm = pl.BlockSpec(memory_space=pltpu.HBM)
    return pl.pallas_call(
        slab_kernel,
        out_shape=jax.ShapeDtypeStruct(shape, p3.dtype),
        in_specs=[in_hbm],
        out_specs=in_hbm,
        scratch_shapes=[
            pltpu.VMEM(p3.shape, p3.dtype),
            pltpu.VMEM(shape, p3.dtype),
            pltpu.SemaphoreType.DMA((2,)),
            pltpu.SemaphoreType.DMA((2,)),
        ],
    )(p3)


def exponent_of(largest):
    return jnp.round(jnp.log2(jnp.clip(largest, 2.0**-100, 2.0**100)))


def fold_kernel(sector_count, out_rows, blk_ref, lane_ref, slab_ref, *refs):
    edge_refs, out_ref, total_ref = refs[:-2], refs[-2], refs[-1]
    peers = lane_ref.shape[0]
    sources, _, cols = slab_ref.shape
    cols, blk_count = cols // 2, sources // peers
    place = {n: k for k, n in enumerate(ring_of(sources))}
    order = [lax.rem(blk_ref[0] + blk_count - k, blk_count) for k in range(blk_count)]
    for d in range(peers):
        places = [place[d * blk_count + j] for j in range(blk_count)]
        left = []
        for j in order:
            n = places[0]
            for k in range(1, blk_count):
                n = jnp.where(j == k, places[k], n)
            left.append(slab_ref[n])
        left = jnp.concatenate(left, axis=0).T
        left = jnp.concatenate([left[:cols], left[cols:]], axis=1)
        lane = lane_ref[d]
        rows = []
        for b in range(sector_count):
            chosen = (lane == b).astype(jnp.float32).astype(left.dtype)
            rows.append(left * chosen)
        right = jnp.concatenate([e[d] for e in edge_refs], axis=0)
        part = jnp.dot(jnp.concatenate(rows, axis=0), right, preferred_element_type=jnp.float32)
        if d == 0:
            total_ref[...] = part
        else:
            total_ref[...] += part
    exponent = exponent_of(jnp.max(jnp.abs(total_ref[...]), axis=(0, 1), keepdims=True))
    scale = jnp.exp2(TOP - exponent)
    lanes = out_ref.shape[2]
    parts = total_ref.shape[1] // lanes
    dests = out_ref.shape[0]
    for n in range(dests):
        place = ring_of(dests).index(n)
        for k in range(parts):
            out_ref[place, k * out_rows : (k + 1) * out_rows] = (
                total_ref[n * out_rows : (n + 1) * out_rows, k * lanes : (k + 1) * lanes] * scale
            )
        out_ref[place, parts * out_rows :] = jnp.broadcast_to(exponent, (NOTE_ROWS, lanes))


def fold_tiles(slabs, edges, lanes, my_blk, sector_count, out_rows):
    sources, depth, cols = slabs.shape
    peers, _, width = edges[0].shape
    cols, blk_count = cols // 2, sources // peers
    dests = sector_count * cols // out_rows
    part_width = 128 if width % 128 == 0 else width
    parts = width // part_width
    shape = (dests, parts * out_rows + NOTE_ROWS, part_width)
    if depth * blk_count % 128 or depth % 16 or cols % 64 or out_rows % 16:
        order = (my_blk - jnp.arange(blk_count)) % blk_count
        left = jnp.take(slabs, np.argsort(ring_of(sources)), axis=0)
        left = left.reshape(peers, blk_count, depth, 2, cols)
        left = jnp.take(left, order, axis=1)
        left = left.transpose(0, 4, 3, 1, 2).reshape(peers, 1, cols, 2 * blk_count * depth)
        labels = jnp.arange(sector_count, dtype=jnp.int32)[None, :, None, None]
        left = left * (lanes[:, :, None, :] == labels).astype(left.dtype)
        right = jnp.concatenate(edges, axis=1)
        total = jnp.einsum("dbsk,dku->bsu", left, right, preferred_element_type=jnp.float32)
        exponent = exponent_of(jnp.max(jnp.abs(total)))
        total = total.reshape(dests, out_rows, parts, part_width) * jnp.exp2(TOP - exponent)
        total = jnp.swapaxes(total, 1, 2).reshape(dests, parts * out_rows, part_width)
        note = jnp.full((dests, NOTE_ROWS, part_width), exponent)
        return jnp.take(jnp.concatenate([total, note], axis=1), np.array(ring_of(dests)), axis=0)
    in_vmem = pl.BlockSpec(memory_space=pltpu.VMEM)
    return pl.pallas_call(
        functools.partial(fold_kernel, sector_count, out_rows),
        out_shape=jax.ShapeDtypeStruct(shape, jnp.float32),
        in_specs=[pl.BlockSpec(memory_space=pltpu.SMEM)] + [in_vmem] * (2 + len(edges)),
        out_specs=in_vmem,
        scratch_shapes=[pltpu.VMEM((sector_count * cols, width), jnp.float32)],
        compiler_params=pltpu.CompilerParams(vmem_limit_bytes=VMEM_LIMIT),
    )(my_blk.reshape(1), lanes, slabs, *edges)


def local(corner, edge_tiles, projector, sector_of):
    sec_count, blk_count = lax.axis_size("sec"), lax.axis_size("blk")
    me, my_blk = lax.axis_index("sec"), lax.axis_index("blk")
    tile_count, tile_rows, width = edge_tiles.shape
    columns = sec_count // 2
    per_peer = tile_count // sec_count
    slab_depth = per_peer * tile_rows
    corner_rows = corner.shape[0]
    sector_count = corner_rows * sec_count // width
    out_rows = corner_rows // blk_count
    spread = columns // sector_count
    sibling = [(i, i ^ 1) for i in range(sec_count)]

    def turn(array, by):
        return lax.ppermute(array, "blk", [(j, (j + by) % blk_count) for j in range(blk_count)])

    edges3 = edge_tiles.reshape(sec_count, slab_depth, width)
    edge_turns = [edges3] + [turn(edges3, k) for k in range(1, blk_count)]
    sectors = jnp.stack([sector_of] + [turn(sector_of, k) for k in range(1, blk_count)])
    lanes = jnp.stack([sectors, lax.ppermute(sectors, "sec", sibling)])
    lanes = jnp.moveaxis(lanes.reshape(2 * blk_count, sec_count, per_peer), 1, 0)
    lanes = jnp.repeat(lanes.reshape(sec_count, 1, -1), tile_rows, axis=2)
    others = [lax.ppermute(edges3, "sec", sibling)]
    edge_turns, lanes = lax.optimization_barrier((edge_turns, lanes))
    others += [lax.ppermute(e, "sec", sibling) for e in edge_turns[1:]]

    slabs = make_slabs(projector, columns, blk_count, out_rows)
    arrived = lax.all_to_all(
        slabs,
        ("sec", "blk"),
        split_axis=0,
        concat_axis=0,
        tiled=True,
        axis_index_groups=[ring_of(sec_count * blk_count)],
    )

    partial = fold_tiles(arrived, edge_turns + others, lanes, my_blk, sector_count, out_rows)
    groups = [[2 * n + c for n in ring_of(columns)] for c in range(2)]
    received = lax.all_to_all(
        partial.astype(jnp.float16),
        "sec",
        split_axis=0,
        concat_axis=0,
        tiled=True,
        axis_index_groups=groups,
    ).astype(jnp.float32)
    scales = jnp.exp2(received[:, -1:] - TOP)
    rows = jnp.sum(received[:, :-NOTE_ROWS] * scales, axis=0)
    rows = jnp.concatenate(jnp.split(rows, rows.shape[0] // out_rows), axis=1)

    share = 2 * spread
    place = me % share
    block = jnp.zeros((share, corner_rows, width), corner.dtype)
    for k in range(share):
        ring = [(i, i // share * share + (i % share + k) % share) for i in range(sec_count)]
        piece = corner if k == 0 else lax.ppermute(corner, "sec", ring)
        block = lax.dynamic_update_index_in_dim(block, piece, (place - k) % share, 0)
    block = block.reshape(width, width)
    high = lax.reduce_precision(rows, exponent_bits=8, mantissa_bits=7)
    both = jnp.concatenate([high, rows - high], axis=1).astype(jnp.bfloat16)
    twice = jnp.concatenate([block, block], axis=0)
    return jnp.dot(both, twice, preferred_element_type=jnp.float32)


def solution(mesh):
    in_specs = (
        P("sec", None),
        P(("sec", "blk"), None, None),
        P(("sec", "blk"), None, None),
        P(("sec", "blk")),
    )
    out_specs = P(("sec", "blk"), None)
    return jax.shard_map(local, mesh=mesh, in_specs=in_specs, out_specs=out_specs, check_vma=False)
```
